256 devices in a mesh: row: 64 (over z, x, core), col: 4 (over y).
Axes of the slice: x: 4, y: 4, z: 8, core: 2. Of those that a mesh axis runs over, the one named last changes fastest.
Arguments:
- student_states: bfloat16 [16384, 4096], P('row', 'col'), may hold values from -24 to 24
- student_proj: bfloat16 [2048, 4096], P('row', 'col'), may hold values from -0.09375 to 0.09375
- teacher_states: bfloat16 [1024, 4096], P('col', 'row'), may hold values from -6 to 6
- teacher_proj: bfloat16 [2048, 4096], P('col', 'row'), may hold values from -0.09375 to 0.09375
Outputs:
- grad_student: float32 [2048, 4096], P('row', 'col')
- grad_teacher: float32 [2048, 4096], P('col', 'row')
The draws below stay inside these ranges and needn't reach their ends.
All inputs are finite; a program needn't handle non-finite values.
Results may differ from the reference program's by a relative error of at most 0.014.
The reference program's roundings to bfloat16 on the way (of `student_emb`, `teacher_emb`, `adjoint_low`, `student_adj` and `teacher_adj`) count: a program that leaves them out, or rounds other values in their place, can miss the bound.
Values may be sent and summed in bfloat16 or wider, within the bound.
A program may use at most 64 MiB of HBM per device.

```python
import math
import jax
import jax.numpy as jnp
from jax import lax

DS = 4096
DT = 4096
E = 2048
ITERS = 3
NS = 16384
NT = 1024


def draw_student_states(key, part):
    key = jax.random.fold_in(key, 7)
    entry_key = jax.random.fold_in(key, 0)
    values = jnp.clip(jax.random.normal(entry_key, (NS, DS), jnp.float32), -6.0, 6.0)
    return values.astype(jnp.bfloat16)


def shard_levels(rng, extent, cuts, low, largest):
    level = 1.0
    for position, blocks in cuts:
        steps = jax.random.uniform(jax.random.fold_in(jax.random.fold_in(rng, 6), position), (blocks,), jnp.float32, low / len(cuts), largest / len(cuts))
        level = level * jnp.repeat(jnp.exp(steps), extent[position] // blocks).reshape((-1,) + (1,) * (len(extent) - 1 - position))
    return level


def normal_values(rng, dims, scale, bound, cuts=(), dtype=jnp.bfloat16):
    entries = scale * jax.random.normal(rng, dims, jnp.float32)
    if cuts:
        entries = entries * shard_levels(rng, dims, cuts, -0.22, 0.18)
    return jnp.clip(entries, -bound, bound).astype(dtype)


def setup_inputs(seed: int = 0) -> dict:
    key_of = jax.random.split(jax.random.key(seed), 5)
    return {
        "student_states": draw_student_states(jax.random.fold_in(key_of[4], 71), 0),
        "student_proj": normal_values(key_of[1], (E, DS), DS ** -0.5, 0.09375, ((0, 64), (1, 4))),
        "teacher_states": normal_values(key_of[2], (NT, DT), 1.0, 6.0, ((0, 4), (1, 64))),
        "teacher_proj": normal_values(key_of[3], (E, DT), DT ** -0.5, 0.09375, ((0, 4), (1, 64))),
    }


TEMPER = 50.0
RIGHT_CONTRACT = (((1,), (1,)), ((), ()))

def lse_rows(values):
    maxima = lax.optimization_barrier(jnp.max(values, axis=1))
    return maxima + jnp.log(lax.optimization_barrier(jnp.sum(jnp.exp(values - maxima[:, None]), axis=1)))

def lse_cols(values):
    maxima = lax.optimization_barrier(jnp.max(values, axis=0))
    return maxima + jnp.log(lax.optimization_barrier(jnp.sum(jnp.exp(values - maxima[None, :]), axis=0)))

def reference(student_states, student_proj, teacher_states, teacher_proj):
    student_emb = lax.dot_general(student_states, student_proj, RIGHT_CONTRACT, preferred_element_type=jnp.float32).astype(jnp.bfloat16)
    teacher_emb = lax.dot_general(teacher_states, teacher_proj, RIGHT_CONTRACT, preferred_element_type=jnp.float32).astype(jnp.bfloat16)
    norm_student = lax.optimization_barrier(jnp.sum(jnp.square(student_emb.astype(jnp.float32)), axis=1))
    norm_teacher = lax.optimization_barrier(jnp.sum(jnp.square(teacher_emb.astype(jnp.float32)), axis=1))
    inverse_temp = TEMPER / E
    cross = jnp.dot(student_emb, teacher_emb.T, preferred_element_type=jnp.float32)
    logits = inverse_temp * (2.0 * cross - norm_student[:, None] - norm_teacher[None, :])
    col_pots = [jnp.zeros((NT,), jnp.float32)]
    row_pots = []
    for sweep in range(ITERS):
        row_pot = -lse_rows(logits + col_pots[-1][None, :])
        row_pots.append(row_pot)
        col_pots.append(-lse_cols(logits + row_pot[:, None]))
    weight = math.sqrt(NS) / NT
    plan = jnp.exp(logits + row_pots[-1][:, None] + col_pots[-1][None, :])
    loss_term = -weight * plan * logits
    col_grad = lax.optimization_barrier(jnp.sum(loss_term, axis=0))
    adjoint = loss_term - weight * plan - plan * col_grad[None, :]
    row_grad = lax.optimization_barrier(jnp.sum(loss_term - plan * col_grad[None, :], axis=1))
    for sweep in range(ITERS - 1, -1, -1):
        flow_term = jnp.exp(logits + row_pots[sweep][:, None] + col_pots[sweep][None, :]) * row_grad[:, None]
        adjoint = adjoint - flow_term
        if sweep > 0:
            col_grad = -lax.optimization_barrier(jnp.sum(flow_term, axis=0))
            back_term = jnp.exp(logits + row_pots[sweep - 1][:, None] + col_pots[sweep][None, :]) * col_grad[None, :]
            adjoint = adjoint - back_term
            row_grad = -lax.optimization_barrier(jnp.sum(back_term, axis=1))
    adjoint_low = adjoint.astype(jnp.bfloat16)
    student_adj = 2.0 * inverse_temp * (jnp.dot(adjoint_low, teacher_emb, preferred_element_type=jnp.float32) - lax.optimization_barrier(jnp.sum(adjoint, axis=1))[:, None] * student_emb.astype(jnp.float32))
    student_adj = student_adj.astype(jnp.bfloat16)
    teacher_adj = 2.0 * inverse_temp * (jnp.dot(adjoint_low.T, student_emb, preferred_element_type=jnp.float32) - lax.optimization_barrier(jnp.sum(adjoint, axis=0))[:, None] * teacher_emb.astype(jnp.float32))
    teacher_adj = teacher_adj.astype(jnp.bfloat16)
    grad_student = jnp.dot(student_adj.T, student_states, preferred_element_type=jnp.float32)
    grad_teacher = jnp.dot(teacher_adj.T, teacher_states, preferred_element_type=jnp.float32)
    return (grad_student, grad_teacher)
```

```python
import math

import jax
import jax.numpy as jnp
from jax import lax
from jax.experimental import pallas as pl
from jax.experimental.pallas import tpu as pltpu
from jax.sharding import PartitionSpec as P

MESH = pl.DeviceIdType.MESH
WEIGHT = math.sqrt(16384) / 1024


def coords():
    r = lax.axis_index("row")
    y = lax.axis_index("col")
    c = lax.rem(r, 2)
    x = lax.rem(r // 2, 4)
    z = r // 8
    return x, y, z, c


def dev(x, y, z, c):
    return ((z * 4 + x) * 2 + c, y)


def partner(stage, i, pos):
    x, y, z, c = pos
    if stage == 0:
        q = lax.rem(x * 4 + y + i, 16)
        return dev(q // 4, lax.rem(q, 4), z, c), q
    q = lax.rem(z * 2 + c + i, 16)
    return dev(x, y, q // 2, lax.rem(q, 2)), q


def sink_kernel(logits_ref, adj_ref, sbuf, rbuf, send_sem, recv_sem):
    pos = coords()
    x, y, z, c = pos
    mine = (x * 4 + y, z * 2 + c)
    barrier = pltpu.get_barrier_semaphore()

    for stage in range(2):
        def greet(i, carry):
            target, _ = partner(stage, i, pos)
            pl.semaphore_signal(barrier, inc=1, device_id=target, device_id_type=MESH)
            return carry
        lax.fori_loop(1, 16, greet, 0)
    pl.semaphore_wait(barrier, 30)

    def start(k, stage, n):
        def body(i, carry):
            target, _ = partner(stage, i, pos)
            pltpu.make_async_remote_copy(
                src_ref=sbuf.at[k, stage, pl.ds(0, n)],
                dst_ref=rbuf.at[k, stage, mine[stage], pl.ds(0, n)],
                send_sem=send_sem.at[k, stage],
                recv_sem=recv_sem.at[k, stage],
                device_id=target,
                device_id_type=MESH,
            ).start()
            return carry
        lax.fori_loop(1, 16, body, 0)

    def arrive(k, stage, n):
        ref = rbuf.at[k, stage, pl.ds(0, 15), pl.ds(0, n)]
        pltpu.make_async_copy(ref, ref, recv_sem.at[k, stage]).wait()

    def pack(k, stage, q, row):
        for j in range(8):
            sbuf[k, stage, q, pl.ds(j, 1), :] = row[:, j * 128:(j + 1) * 128]

    def unpack(k, q):
        return jnp.concatenate([sbuf[k, 2, q, pl.ds(j, 1), :] for j in range(8)], axis=1)

    def reduce_sum(k, row):
        pack(k, 0, 0, row)
        for stage in range(2):
            start(k, stage, 1)
            rbuf[k, stage, mine[stage], 0] = sbuf[k, stage, 0]
            arrive(k, stage, 1)
            sbuf[k, stage + 1, 0] = jnp.sum(rbuf[k, stage, :, 0], axis=0)
        return unpack(k, 0)

    def reduce_lse(k, top, total):
        pack(k, 0, 0, top)
        pack(k, 0, 1, total)
        for stage in range(2):
            start(k, stage, 2)
            rbuf[k, stage, mine[stage], pl.ds(0, 2)] = sbuf[k, stage, pl.ds(0, 2)]
            arrive(k, stage, 2)
            tops = rbuf[k, stage, :, 0]
            best = jnp.max(tops, axis=0)
            sbuf[k, stage + 1, 0] = best
            sbuf[k, stage + 1, 1] = jnp.sum(
                rbuf[k, stage, :, 1] * jnp.exp(tops - best[None]), axis=0)
        sbuf[k, 2, 0] = -(sbuf[k, 2, 0] + jnp.log(sbuf[k, 2, 1]))
        return unpack(k, 0)

    def reduce_last(k, top, total, moment):
        pack(k, 0, 0, top)
        pack(k, 0, 1, total)
        pack(k, 0, 2, moment)
        for stage in range(2):
            start(k, stage, 3)
            rbuf[k, stage, mine[stage]] = sbuf[k, stage]
            arrive(k, stage, 3)
            tops = rbuf[k, stage, :, 0]
            best = jnp.max(tops, axis=0)
            scale = jnp.exp(tops - best[None])
            sbuf[k, stage + 1, 0] = best
            sbuf[k, stage + 1, 1] = jnp.sum(rbuf[k, stage, :, 1] * scale, axis=0)
            sbuf[k, stage + 1, 2] = jnp.sum(rbuf[k, stage, :, 2] * scale, axis=0)
        sbuf[k, 2, 0] = -(sbuf[k, 2, 0] + jnp.log(sbuf[k, 2, 1]))
        sbuf[k, 2, 2] = -WEIGHT * sbuf[k, 2, 2] / sbuf[k, 2, 1]
        return unpack(k, 0), unpack(k, 2)

    logits = logits_ref[...]
    gs = [None]
    fs = [None]
    for k in range(3):
        v = logits if gs[k] is None else logits + gs[k]
        top = jnp.max(v, axis=1, keepdims=True)
        f = -(top + jnp.log(jnp.sum(jnp.exp(v - top), axis=1, keepdims=True)))
        fs.append(f)
        v = logits + f
        top = jnp.max(v, axis=0, keepdims=True)
        e = jnp.exp(v - top)
        total = jnp.sum(e, axis=0, keepdims=True)
        if k < 2:
            gs.append(reduce_lse(k, top, total))
        else:
            moment = jnp.sum(e * logits, axis=0, keepdims=True)
            g, gbar = reduce_last(k, top, total, moment)
            gs.append(g)
    plan = jnp.exp(logits + fs[3] + gs[3])
    loss = -WEIGHT * plan * logits
    adjoint = loss - WEIGHT * plan - plan * gbar
    fbar = jnp.sum(loss - plan * gbar, axis=1, keepdims=True)
    for k in (3, 2, 1):
        v = logits + fs[k]
        if k > 1:
            v = v + gs[k - 1]
        flow = jnp.exp(v) * fbar
        adjoint = adjoint - flow
        if k > 1:
            gbar = -reduce_sum(6 - k, jnp.sum(flow, axis=0, keepdims=True))
            flow2 = jnp.exp(logits + fs[k - 1] + gs[k - 1]) * gbar
            adjoint = adjoint - flow2
            fbar = -jnp.sum(flow2, axis=1, keepdims=True)
    adj_ref[...] = adjoint
    for stage in range(2):
        for k, n in enumerate((2, 2, 3, 1, 1)):
            ref = rbuf.at[k, stage, pl.ds(0, 15), pl.ds(0, n)]
            pltpu.make_async_copy(ref, ref, send_sem.at[k, stage]).wait()


def sinkhorn(logits):
    return pl.pallas_call(
        sink_kernel,
        out_shape=jax.ShapeDtypeStruct((64, 1024), jnp.float32),
        in_specs=[pl.BlockSpec(memory_space=pltpu.VMEM)],
        out_specs=pl.BlockSpec(memory_space=pltpu.VMEM),
        scratch_shapes=[
            pltpu.VMEM((5, 3, 3, 8, 128), jnp.float32),
            pltpu.VMEM((5, 2, 16, 3, 8, 128), jnp.float32),
            pltpu.SemaphoreType.DMA((5, 2)),
            pltpu.SemaphoreType.DMA((5, 2)),
        ],
        compiler_params=pltpu.CompilerParams(
            collective_id=0, has_side_effects=True, vmem_limit_bytes=32 * 2**20),
        name="sinkhorn",
    )(logits)


RIGHT_CONTRACT = (((1,), (1,)), ((), ()))
LEFT_CONTRACT = (((0,), (0,)), ((), ()))
INVERSE_TEMP = 50.0 / 2048


def per_device(student_states, student_proj, teacher_states, teacher_proj):
    partial_student = lax.dot_general(
        student_states,
        lax.all_gather(student_proj, "row", axis=0, tiled=True),
        RIGHT_CONTRACT,
        preferred_element_type=jnp.float32,
    )
    emb = lax.psum(partial_student, "col").astype(jnp.bfloat16)
    teacher_full = lax.all_gather(teacher_proj, "col", axis=0, tiled=True)
    partial_teacher = lax.dot_general(
        teacher_states, teacher_full, RIGHT_CONTRACT, preferred_element_type=jnp.float32
    )
    teacher_part = lax.psum(partial_teacher, "row").astype(jnp.bfloat16)
    teacher_emb = lax.all_gather(teacher_part, "col", axis=0, tiled=True)
    col = lax.axis_index("col")
    student_emb = lax.dynamic_slice_in_dim(emb, col * 64, 64, 0)
    norm_student = jnp.sum(jnp.square(student_emb.astype(jnp.float32)), axis=1)
    norm_teacher = jnp.sum(jnp.square(teacher_emb.astype(jnp.float32)), axis=1)
    cross = lax.dot_general(
        student_emb, teacher_emb, RIGHT_CONTRACT, preferred_element_type=jnp.float32
    )
    logits = INVERSE_TEMP * (2.0 * cross - norm_student[:, None] - norm_teacher[None, :])
    adjoint = sinkhorn(logits)
    adjoint_low = adjoint.astype(jnp.bfloat16)
    student_adj = (
        2.0
        * INVERSE_TEMP
        * (
            jnp.dot(adjoint_low, teacher_emb, preferred_element_type=jnp.float32)
            - jnp.sum(adjoint, axis=1)[:, None] * student_emb.astype(jnp.float32)
        )
    ).astype(jnp.bfloat16)
    columns = lax.all_gather(student_adj, "col", axis=0, tiled=True)
    grad_student = lax.psum_scatter(
        lax.dot_general(columns, student_states, LEFT_CONTRACT, preferred_element_type=jnp.float32),
        "row",
        scatter_dimension=0,
        tiled=True,
    )
    adjoint_rows = lax.all_to_all(adjoint, "col", split_axis=1, concat_axis=0, tiled=True)
    col_mass = jnp.sum(adjoint_rows, axis=0)
    product = lax.dot_general(
        adjoint_rows.astype(jnp.bfloat16), emb, LEFT_CONTRACT, preferred_element_type=jnp.float32
    )
    teacher_share = lax.psum_scatter(
        2.0 * INVERSE_TEMP * (product - col_mass[:, None] * teacher_part.astype(jnp.float32)),
        "row",
        scatter_dimension=0,
        tiled=True,
    )
    teacher_adj = lax.all_gather(teacher_share.astype(jnp.bfloat16), "row", axis=0, tiled=True)
    grad_teacher = lax.psum_scatter(
        lax.dot_general(
            teacher_adj, teacher_states, LEFT_CONTRACT, preferred_element_type=jnp.float32
        ).astype(jnp.bfloat16),
        "col",
        scatter_dimension=0,
        tiled=True,
    ).astype(jnp.float32)
    return (grad_student, grad_teacher)


def solution(mesh):
    placed = (P("row", "col"), P("row", "col"), P("col", "row"), P("col", "row"))
    return jax.shard_map(
        per_device,
        mesh=mesh,
        in_specs=placed,
        out_specs=(P("row", "col"), P("col", "row")),
        check_vma=False,
    )
```
